32 devices in a mesh: blk: 4 (over y, core), cols: 8 (over z, x).
Axes of the slice: x: 2, y: 2, z: 4, core: 2. Of those that a mesh axis runs over, the one named last changes fastest.
Arguments:
- blocks: bfloat16 [8, 16, 24, 128, 128], P('cols', 'blk'), may hold values from -4 to 4
- columns: int32 [8, 16, 24], P('cols', 'blk'), may hold values from 0 to 127, as said below
- counts: int32 [8, 16], P('cols', 'blk'), may hold values from 12 to 24, as said below
- owners: int32 [8, 16, 1], P('cols', 'blk'), may hold values from 0 to 3; in each aligned block of 4 rows (0 to 3, 4 to 7, ..., all dimensions but the last counted through in order) at most 2 rows name the same one
Outputs:
- squared: bfloat16 [8, 4, 8, 24, 128, 128], P('cols', 'blk')
The draws below stay inside these ranges and needn't reach their ends.
Inputs may be any that keep to these rules, and one draw needn't show every extreme that they name: `columns`: the 24 entries of a block row of slab g are distinct and lie among the 48 block rows of slabs g - 1, g, g + 1, the slab index taken cyclically. `counts`: in every slab some block row has all 24 slots live. `owners`: among the 4 rows of one device each owner appears at most 2 times.
All inputs are finite; a program needn't handle non-finite values.
Results may differ from the reference program's by a relative error of at most 0.001.
Values may be sent and summed in bfloat16 or wider, within the bound.
A program may use at most 192 MiB of HBM per device.

```python
import math
import jax
import jax.numpy as jnp
import numpy as np
from jax import lax

B = 128
K = 24
RD = 4
CAP = 2
G = 16
GROUPS = 8
SLOTS = 8
NBR = 128
N_BLK = 4


def draw_columns(key, part):
    key = jax.random.fold_in(key, 11)
    row_keys = jax.random.split(key, NBR)
    picks = jax.vmap(lambda single: jax.random.permutation(single, 3 * G)[:K])(row_keys)
    start = (jnp.arange(NBR, dtype=jnp.int32) // G - 1) * G
    return jnp.mod(picks.astype(jnp.int32) + start[:, None], NBR).astype(jnp.int32).reshape(GROUPS, G, K)


def draw_counts(key, part):
    key = jax.random.fold_in(key, 12)
    draw_key, spot_key = jax.random.split(key)
    values = jax.random.randint(draw_key, (GROUPS, G), K // 2, K + 1)
    position = jax.random.randint(spot_key, (GROUPS,), 0, G)
    filled = jnp.arange(G, dtype=jnp.int32)[None, :] == position[:, None]
    return jnp.where(filled, K, values).astype(jnp.int32)


def block_scale(key, shape, shards, low, largest):
    level, own = 1.0, jax.random.fold_in(key, 6)
    for dim, shards_of in shards:
        draws = jnp.exp(jax.random.uniform(jax.random.fold_in(own, dim), (shards_of,), jnp.float32, low / len(shards), largest / len(shards)))
        level = level * jnp.repeat(draws, shape[dim] // shards_of).reshape([-1 if axis == dim else 1 for axis in range(len(shape))])
    return level


def routed_block(rng, own, number, rows, count, top, bound, skew):
    sequence = jax.random.permutation(rng, count)
    heavy_load, ordinary = load_shares(count, rows * top, bound, skew, True), load_shares(count, rows * top, bound, skew, False)
    places = jnp.arange(count)

    def named(tallies, rotation):
        used = int((tallies > 0).sum())
        fixed = max(1, used // 4)
        shifted = fixed + (places - fixed + rotation * (used - fixed)) % max(1, count - fixed)
        return jnp.zeros((count,), jnp.int32).at[sequence[jnp.where(places < fixed, places, shifted)]].set(jnp.asarray(tallies, jnp.int32))

    tallies = jnp.where(number % 4 == 0, named(heavy_load, number // 4), named(ordinary, number - number // 4 - 1))
    mixed = jax.random.permutation(jax.random.fold_in(own, 3), count)
    giver, taker = mixed[0:count // 2 * 2:2], mixed[1:count // 2 * 2:2]
    margin = jnp.minimum(tallies[giver] - 1, bound - tallies[taker]) // 2
    margin = jnp.where((giver == sequence[0]) | (taker == sequence[0]) | (tallies[taker] == 0), 0, jnp.maximum(margin, 0))
    shifted = jax.random.randint(jax.random.fold_in(own, 4), (count // 2,), 0, 1 << 20) % (margin + 1)
    tallies = tallies.at[giver].add(-shifted).at[taker].add(shifted)
    items = jnp.searchsorted(jnp.cumsum(tallies), jnp.arange(rows * top), side="right").astype(jnp.int32)
    grid = items.reshape(top, rows).T
    grid = grid[jax.random.permutation(jax.random.fold_in(own, 1), rows)]
    rotation = jax.random.randint(jax.random.fold_in(own, 2), (rows, 1), 0, top)
    return jnp.take_along_axis(grid, (jnp.arange(top)[None, :] + rotation) % top, axis=1)


def load_shares(number_of, total, limit, lean, full):
    weights = [(1 << 20) // math.isqrt(standing ** lean) + 1 for standing in range(1, number_of + 1)]
    largest = limit if full else min(limit, max(-(-total // number_of), total * weights[0] // sum(weights)))
    least = 1 if total - largest >= number_of - 1 else 0
    given, spare = [largest] + [least] * (number_of - 1), total - largest - least * (number_of - 1)
    while spare > 0:
        movable = [i for i in range(1, number_of) if given[i] < largest] or [i for i in range(1, number_of) if given[i] < limit]
        pool, remaining = sum([weights[i] for i in movable]), spare
        for i in movable:
            more = min(limit - given[i], max(1, remaining * weights[i] // pool), spare)
            given[i] = given[i] + more
            spare = spare - more
    return np.array(given)


def scatter_about(key, extent, deviation, limit, pieces=(), held_as=jnp.bfloat16):
    factor_of = block_scale(key, extent, pieces, -0.22, 0.18) if pieces else 1.0
    values = jax.random.normal(key, extent, jnp.float32) * deviation * factor_of
    return jnp.minimum(jnp.maximum(values, -limit), limit).astype(held_as)


def setup_inputs(seed: int = 0) -> dict:
    seeds = jax.random.split(jax.random.key(seed), 5)
    blocks = scatter_about(seeds[0], (GROUPS, G, K, B, B), 0.25, 4.0, ((0, 8), (1, 4)))
    columns = draw_columns(jax.random.fold_in(seeds[4], 71), 0)
    counts = draw_counts(jax.random.fold_in(seeds[4], 71), 0)
    owners_keys = jax.random.split(jax.random.fold_in(seeds[3], 1), GROUPS * G // RD)
    owners_turns = jax.random.permutation(jax.random.fold_in(seeds[3], 3), GROUPS * G // RD)
    owners = jax.vmap(lambda own, number: routed_block(jax.random.fold_in(seeds[3], 2), own, number, RD, N_BLK, 1, CAP, 1))(owners_keys, owners_turns).reshape((GROUPS, G, 1))
    return {"blocks": blocks, "columns": columns, "counts": counts, "owners": owners}


def row_product(left_blocks, left_cols, panel, panel_cols, offset, total_rows):
    window = panel_cols.shape[0]
    is_live = left_cols >= 0
    relative = jnp.mod(left_cols - offset, total_rows).astype(jnp.int32)
    onehot = ((relative[:, None] == jnp.arange(window, dtype=jnp.int32)[None, :]) & is_live[:, None]).astype(jnp.float32)
    dense = jnp.einsum("tw,tab->wab", onehot, left_blocks.astype(jnp.float32))
    chosen = jnp.clip(relative, 0, window - 1)
    partner = panel[chosen].astype(jnp.float32)
    partner_cols = panel_cols[chosen]
    partner_rel = jnp.mod(partner_cols - offset, total_rows).astype(jnp.int32)
    inside = (partner_cols >= 0) & (partner_rel < window)
    matched = dense[jnp.clip(partner_rel, 0, window - 1)]
    matched = jnp.where(inside[:, :, None, None], matched, jnp.zeros((), jnp.float32))
    summed = jnp.einsum("suab,sucb->sac", matched, partner)
    return jnp.where(is_live[:, None, None], summed, jnp.zeros((), jnp.float32)).astype(jnp.bfloat16)


def reference(blocks, columns, counts, owners):
    slot_iota = jnp.arange(K, dtype=jnp.int32)
    marked = jnp.where(slot_iota[None, None, :] < counts[:, :, None], columns, -1).astype(jnp.int32)
    flat_blocks = blocks.reshape(NBR, K, B, B)
    flat_cols = marked.reshape(NBR, K)
    order = jnp.arange(G, dtype=jnp.int32)
    source = order // RD

    def one_group(group):
        offset = ((group - 1) * G).astype(jnp.int32)
        picked = jnp.mod(jnp.arange(3 * G, dtype=jnp.int32) + offset, NBR).astype(jnp.int32)
        panel = flat_blocks[picked]
        panel_cols = flat_cols[picked]

        def one_row(pair):
            return row_product(pair[0], pair[1], panel, panel_cols, offset, NBR)

        products = lax.map(one_row, (blocks[group], marked[group]))
        owner_vec = owners[group, :, 0].astype(jnp.int32)
        same = (owner_vec[None, :] == owner_vec[:, None]) & (source[None, :] == source[:, None]) & (order[None, :] < order[:, None])
        rank = jnp.sum(same.astype(jnp.int32), axis=1)
        target = owner_vec * SLOTS + source * CAP + rank
        select = (target[None, :] == jnp.arange(N_BLK * SLOTS, dtype=jnp.int32)[:, None]).astype(jnp.float32)
        placed = jnp.einsum("ni,ikab->nkab", select, products.astype(jnp.float32))
        return placed.reshape(N_BLK, SLOTS, K, B, B).astype(jnp.bfloat16)

    return lax.map(one_group, jnp.arange(GROUPS, dtype=jnp.int32))
```

```python
import functools

import jax
import jax.numpy as jnp
from jax import lax
from jax.experimental import pallas as pl
from jax.experimental.pallas import tpu as pltpu
from jax.sharding import PartitionSpec as P

CAP = 2
DEPTH = 4
TOGETHER = 4
CODE = 4096
VIA_PAIR = 2
VIA_FAR = 2
MESH = pl.DeviceIdType.MESH

OWN, PAIR, FAR = 0, 1, 2


def gather_kernel(ngroups, rows_dev, blocks_ref, panel_ref, send_sem, recv_sem, own_sem):
    g = lax.axis_index("cols")
    j = lax.axis_index("blk")
    odd = g % 2
    core = j % 2
    side = j // 2
    pair = g + 1 - 2 * odd
    ahead = (g + 2 - 4 * odd + ngroups) % ngroups
    behind = (g - 2 + 4 * odd + ngroups) % ngroups
    slab = {OWN: 1, PAIR: 2 - 2 * odd, FAR: 2 * odd}
    member = {
        0: j,
        1: side * 2 + 1 - core,
        2: (1 - side) * 2 + core,
        3: (1 - side) * 2 + 1 - core,
    }
    device = {
        "core": (g, member[1]),
        "side": (g, member[2]),
        "pair": (pair, j),
        "ahead": (ahead, j),
    }

    barrier = pltpu.get_barrier_semaphore()
    partners = list(device.values()) + [(behind, j)]
    for to_g, to_j in partners:
        pl.semaphore_signal(
            barrier, inc=1, device_id={"cols": to_g, "blk": to_j}, device_id_type=MESH
        )
    pl.semaphore_wait(barrier, len(partners))

    pending = []

    def place(kind, who, m):
        return panel_ref.at[slab[kind], member[who] * rows_dev + m]

    def copy(kind, who, m, to, there_kind, there_who):
        src = blocks_ref.at[0, m] if (kind, who) == (OWN, 0) else place(kind, who, m)
        slab_there = slab[FAR] if to in ("pair", "ahead") else slab[kind]
        to_g, to_j = device[to]
        made = pltpu.make_async_remote_copy(
            src_ref=src,
            dst_ref=panel_ref.at[slab_there, member[who] * rows_dev + m],
            send_sem=send_sem.at[there_kind, there_who, m],
            recv_sem=recv_sem.at[there_kind, there_who, m],
            device_id={"cols": to_g, "blk": to_j},
            device_id_type=MESH,
        )
        made.start()
        pending.append(made)

    def arrived(kind, who, m):
        pltpu.make_async_copy(
            place(kind, who, m), place(kind, who, m), recv_sem.at[kind, who, m]
        ).wait()

    for m in range(rows_dev):
        copy(OWN, 0, m, "pair", PAIR, 0)
        copy(OWN, 0, m, "side", OWN, 2)
        copy(OWN, 0, m, "core", OWN, 1)
    own = pltpu.make_async_copy(
        blocks_ref.at[0], panel_ref.at[1, pl.ds(j * rows_dev, rows_dev)], own_sem
    )
    own.start()

    for step in range(rows_dev + 2):
        if step < rows_dev:
            m = step
            arrived(PAIR, 0, m)
            copy(PAIR, 0, m, "ahead", FAR, 0)
            if m >= VIA_PAIR:
                copy(PAIR, 0, m, "side", PAIR, 2)
            copy(PAIR, 0, m, "core", PAIR, 1)
            arrived(OWN, 2, m)
            if m < VIA_PAIR:
                copy(OWN, 2, m, "pair", PAIR, 2)
            copy(OWN, 2, m, "core", OWN, 3)
        if 0 <= step - 1 < rows_dev:
            m = step - 1
            arrived(FAR, 0, m)
            if m >= VIA_FAR:
                copy(FAR, 0, m, "side", FAR, 2)
            copy(FAR, 0, m, "core", FAR, 1)
            arrived(PAIR, 2, m)
            if m < VIA_FAR:
                copy(PAIR, 2, m, "ahead", FAR, 2)
            copy(PAIR, 2, m, "core", PAIR, 3)
        if 0 <= step - 2 < rows_dev:
            m = step - 2
            arrived(FAR, 2, m)
            copy(FAR, 2, m, "core", FAR, 3)
    for kind in (OWN, PAIR, FAR):
        for who in (1, 3):
            for m in range(rows_dev):
                arrived(kind, who, m)
    for made in pending:
        made.wait_send()
    own.wait()


def gather_panel(blocks, ngroups, group_rows):
    rows_dev, stored, width = blocks.shape[1:4]
    return pl.pallas_call(
        functools.partial(gather_kernel, ngroups, rows_dev),
        out_shape=jax.ShapeDtypeStruct((3, group_rows, stored, width, width), blocks.dtype),
        in_specs=[pl.BlockSpec(memory_space=pl.ANY)],
        out_specs=pl.BlockSpec(memory_space=pl.ANY),
        scratch_shapes=[
            pltpu.SemaphoreType.DMA((3, 4, rows_dev)),
            pltpu.SemaphoreType.DMA((3, 4, rows_dev)),
            pltpu.SemaphoreType.DMA,
        ],
        compiler_params=pltpu.CompilerParams(collective_id=0, has_side_effects=True),
        name="gather_panel",
    )(blocks)


def product_kernel(total, stored, trips_ref, pairs_ref, panel_hbm, out_ref, panel, sem):
    slot = pl.program_id(0)
    width = panel.shape[1]

    @pl.when(slot == 0)
    def _():
        fetch = pltpu.make_async_copy(panel_hbm, panel.at[pl.ds(0, total)], sem)
        fetch.start()
        panel[total] = jnp.zeros((width, width), panel.dtype)
        fetch.wait()

    bunches = stored // TOGETHER

    def one_bunch(bunch, carry):
        first = bunch * TOGETHER

        def step(trip, sums):
            new = []
            for n in range(TOGETHER):
                lefts, rights = [], []
                for d in range(DEPTH):
                    code = pairs_ref[slot * stored + first + n, trip * DEPTH + d]
                    lefts.append(panel[code % CODE])
                    rights.append(panel[code // CODE])
                new.append(
                    sums[n]
                    + lax.dot_general(
                        jnp.concatenate(lefts, axis=1),
                        jnp.concatenate(rights, axis=1),
                        (((1,), (1,)), ((), ())),
                        preferred_element_type=jnp.float32,
                    )
                )
            return tuple(new)

        zero = jnp.zeros((width, width), jnp.float32)
        sums = lax.fori_loop(0, trips_ref[slot, bunch], step, (zero,) * TOGETHER)
        for n in range(TOGETHER):
            out_ref[0, 0, 0, first + n] = sums[n].astype(out_ref.dtype)
        return carry

    lax.fori_loop(0, bunches, one_bunch, 0)


def products(panel, trips, pairs, slots):
    total, width = panel.shape[0], panel.shape[1]
    stored = pairs.shape[1]
    return pl.pallas_call(
        functools.partial(product_kernel, total, stored),
        out_shape=jax.ShapeDtypeStruct((1, 1, slots, stored, width, width), panel.dtype),
        grid_spec=pltpu.PrefetchScalarGridSpec(
            num_scalar_prefetch=2,
            grid=(slots,),
            in_specs=[pl.BlockSpec(memory_space=pl.ANY)],
            out_specs=pl.BlockSpec(
                (1, 1, 1, stored, width, width), lambda slot, *_: (0, 0, slot, 0, 0, 0)
            ),
            scratch_shapes=[
                pltpu.VMEM((total + 1, width, width), panel.dtype),
                pltpu.SemaphoreType.DMA,
            ],
        ),
        compiler_params=pltpu.CompilerParams(vmem_limit_bytes=50 * 1024 * 1024),
        name="products",
    )(trips, pairs, panel)


def work_lists(meta, ngroups, group_rows, rows_dev, stored, nblk):
    g = lax.axis_index("cols")
    me = lax.axis_index("blk")
    total_rows = ngroups * group_rows
    window = 3 * group_rows
    offset = (g - 1) * group_rows
    near = jnp.take(meta, jnp.mod(jnp.arange(window) + offset, total_rows), axis=0)
    cols = near[:, :stored]
    rel = jnp.mod(cols - offset, total_rows)
    rel = jnp.where((cols >= 0) & (rel < window), rel, -1)
    owner = near[group_rows : 2 * group_rows, stored].reshape(nblk, rows_dev)
    mine = owner == me
    order = jnp.arange(rows_dev)
    rank = jnp.sum(mine[:, None, :] & (order[None, None, :] < order[None, :, None]), axis=2)
    hit = mine[:, None, :] & (rank[:, None, :] == jnp.arange(CAP)[None, :, None])
    row = jnp.arange(nblk * rows_dev).reshape(nblk, 1, rows_dev)
    slot_row = jnp.max(jnp.where(hit, row, -1), axis=2).reshape(nblk * CAP)
    left_row = group_rows + jnp.maximum(slot_row, 0)
    left = jnp.where(slot_row[:, None] >= 0, jnp.take(rel, left_row, axis=0), -1)
    partner = jnp.maximum(left, 0)
    right = jnp.where(left[:, :, None] >= 0, jnp.take(rel, partner, axis=0), -1)
    step = jnp.arange(stored)
    same = (right[:, :, :, None] == left[:, None, None, :]) & (right[:, :, :, None] >= 0)
    found = jnp.max(jnp.where(same, step, -1), axis=3)
    match = found >= 0
    place = jnp.sum(match[:, :, None, :] & (step[None, :] < step[:, None]), axis=3)
    code = (left_row[:, None, None] * stored + found) + CODE * (
        partner[:, :, None] * stored + step
    )
    pad = window * stored
    at = match[:, :, None, :] & (place[:, :, None, :] == step[:, None])
    pairs = jnp.max(jnp.where(at, code[:, :, None, :], -1), axis=3)
    pairs = jnp.where(pairs >= 0, pairs, pad)
    count = jnp.sum(match, axis=2)
    most = jnp.max(count.reshape(nblk * CAP, stored // TOGETHER, TOGETHER), axis=2)
    trips = (most + DEPTH - 1) // DEPTH
    return trips.astype(jnp.int32), pairs.reshape(-1, stored).astype(jnp.int32)


def local(blocks, columns, counts, owners, *, nblk, ngroups):
    rows_dev, stored, width = blocks.shape[1:4]
    group_rows = nblk * rows_dev
    slot_iota = jnp.arange(stored, dtype=jnp.int32)
    marked = jnp.where(slot_iota[None, None, :] < counts[:, :, None], columns, -1)
    meta = jnp.concatenate([marked[0], owners[0]], axis=1)
    meta = lax.all_gather(meta, ("cols", "blk"), axis=0, tiled=True)
    panel = gather_panel(blocks, ngroups, group_rows)
    trips, pairs = work_lists(meta, ngroups, group_rows, rows_dev, stored, nblk)
    panel = panel.reshape(3 * group_rows * stored, width, width)
    return products(panel, trips, pairs, nblk * CAP)


def solution(mesh):
    placed = (
        P("cols", "blk", None, None, None),
        P("cols", "blk", None),
        P("cols", "blk"),
        P("cols", "blk", None),
    )
    return jax.shard_map(
        functools.partial(local, nblk=mesh.shape["blk"], ngroups=mesh.shape["cols"]),
        mesh=mesh,
        in_specs=placed,
        out_specs=P("cols", "blk", None, None, None, None),
        check_vma=False,
    )
```

```python
import functools

import jax
import jax.numpy as jnp
from jax import lax
from jax.experimental import pallas as pl
from jax.experimental.pallas import tpu as pltpu
from jax.sharding import PartitionSpec as P

CAP = 2
DEPTH = 4
TOGETHER = 4
SHIFT = 12
ROWS, LANES = 8, 128
VIA_PAIR = 2
VIA_FAR = 2
MESH = pl.DeviceIdType.MESH

OWN, PAIR, FAR = 0, 1, 2


def gather_kernel(
    ngroups, rows_dev, blocks_ref, meta_ref, panel_ref, near_ref, send_sem, recv_sem, own_sem
):
    g = lax.axis_index("cols")
    j = lax.axis_index("blk")
    odd = g % 2
    core = j % 2
    side = j // 2
    pair = g + 1 - 2 * odd
    ahead = (g + 2 - 4 * odd + ngroups) % ngroups
    behind = (g - 2 + 4 * odd + ngroups) % ngroups
    slab = {OWN: 1, PAIR: 2 - 2 * odd, FAR: 2 * odd}
    member = {
        0: j,
        1: side * 2 + 1 - core,
        2: (1 - side) * 2 + core,
        3: (1 - side) * 2 + 1 - core,
    }
    device = {
        "core": (g, member[1]),
        "side": (g, member[2]),
        "pair": (pair, j),
        "ahead": (ahead, j),
    }

    barrier = pltpu.get_barrier_semaphore()
    partners = list(device.values()) + [(behind, j)]
    for to_g, to_j in partners:
        pl.semaphore_signal(
            barrier, inc=1, device_id={"cols": to_g, "blk": to_j}, device_id_type=MESH
        )
    pl.semaphore_wait(barrier, len(partners))

    pending = []

    def place(kind, who, m):
        if m == rows_dev:
            return near_ref.at[slab[kind], member[who]]
        return panel_ref.at[slab[kind], member[who] * rows_dev + m]

    def copy(kind, who, m, to, there_kind, there_who):
        slab_there = slab[FAR] if to in ("pair", "ahead") else slab[kind]
        if m == rows_dev:
            mine, there = meta_ref, near_ref.at[slab_there, member[who]]
        else:
            mine = blocks_ref.at[0, m]
            there = panel_ref.at[slab_there, member[who] * rows_dev + m]
        src = mine if (kind, who) == (OWN, 0) else place(kind, who, m)
        to_g, to_j = device[to]
        made = pltpu.make_async_remote_copy(
            src_ref=src,
            dst_ref=there,
            send_sem=send_sem.at[there_kind, there_who, m],
            recv_sem=recv_sem.at[there_kind, there_who, m],
            device_id={"cols": to_g, "blk": to_j},
            device_id_type=MESH,
        )
        made.start()
        pending.append(made)

    def arrived(kind, who, m):
        pltpu.make_async_copy(
            place(kind, who, m), place(kind, who, m), recv_sem.at[kind, who, m]
        ).wait()

    order = [rows_dev] + list(range(rows_dev))
    for m in order:
        copy(OWN, 0, m, "pair", PAIR, 0)
        copy(OWN, 0, m, "side", OWN, 2)
        copy(OWN, 0, m, "core", OWN, 1)
    local_copies = [
        pltpu.make_async_copy(
            blocks_ref.at[0], panel_ref.at[1, pl.ds(j * rows_dev, rows_dev)], own_sem.at[0]
        ),
        pltpu.make_async_copy(meta_ref, near_ref.at[1, j], own_sem.at[1]),
    ]
    for made in local_copies:
        made.start()

    def first(m):
        arrived(PAIR, 0, m)
        copy(PAIR, 0, m, "ahead", FAR, 0)
        if m >= VIA_PAIR:
            copy(PAIR, 0, m, "side", PAIR, 2)
        copy(PAIR, 0, m, "core", PAIR, 1)
        arrived(OWN, 2, m)
        if m < VIA_PAIR:
            copy(OWN, 2, m, "pair", PAIR, 2)
        copy(OWN, 2, m, "core", OWN, 3)

    def second(m):
        arrived(FAR, 0, m)
        if m >= VIA_FAR:
            copy(FAR, 0, m, "side", FAR, 2)
        copy(FAR, 0, m, "core", FAR, 1)
        arrived(PAIR, 2, m)
        if m < VIA_FAR:
            copy(PAIR, 2, m, "ahead", FAR, 2)
        copy(PAIR, 2, m, "core", PAIR, 3)

    def third(m):
        arrived(FAR, 2, m)
        copy(FAR, 2, m, "core", FAR, 3)

    for step in range(len(order) + 2):
        for back, stage in enumerate((first, second, third)):
            if 0 <= step - back < len(order):
                stage(order[step - back])
    for kind in (OWN, PAIR, FAR):
        for who in (1, 3):
            for m in order:
                arrived(kind, who, m)
    for made in pending:
        made.wait_send()
    for made in local_copies:
        made.wait()


def gather_panel(blocks, meta, ngroups, group_rows):
    rows_dev, stored, width = blocks.shape[1:4]
    return pl.pallas_call(
        functools.partial(gather_kernel, ngroups, rows_dev),
        out_shape=(
            jax.ShapeDtypeStruct((3, group_rows, stored, width, width), blocks.dtype),
            jax.ShapeDtypeStruct((3, group_rows // rows_dev) + meta.shape, meta.dtype),
        ),
        in_specs=[pl.BlockSpec(memory_space=pl.ANY)] * 2,
        out_specs=[pl.BlockSpec(memory_space=pl.ANY)] * 2,
        scratch_shapes=[
            pltpu.SemaphoreType.DMA((3, 4, rows_dev + 1)),
            pltpu.SemaphoreType.DMA((3, 4, rows_dev + 1)),
            pltpu.SemaphoreType.DMA((2,)),
        ],
        compiler_params=pltpu.CompilerParams(collective_id=0, has_side_effects=True),
        name="gather_panel",
    )(blocks, meta)


def exact_dot(left, right, dims=((1,), (0,))):
    return lax.dot_general(
        left.astype(jnp.bfloat16),
        right.astype(jnp.bfloat16),
        (dims, ((), ())),
        preferred_element_type=jnp.float32,
    )


def work_lists(meta, me, offset, total_rows, rows_dev, stored, nblk):
    held = meta.shape[0]
    window = 3 * nblk * rows_dev
    results = nblk * CAP * stored
    bits = ROWS.bit_length() - 1

    def iota(shape, axis):
        return lax.broadcasted_iota(jnp.int32, shape, axis)

    row = iota((results, 1), 0)
    slot = jnp.zeros_like(row)
    for k in range(1, nblk * CAP):
        slot += (row >= k * stored).astype(jnp.int32)
    source = jnp.zeros_like(row)
    for k in range(1, nblk):
        source += (slot >= k * CAP).astype(jnp.int32)
    turn = slot - CAP * source
    item = row - slot * stored
    lane = iota((results, LANES), 1)
    at = iota((results, held), 1)
    shard = at >> bits
    within = at & (ROWS - 1)
    index = shard * rows_dev + within

    picks = (lane == stored).astype(jnp.float32)
    owner = exact_dot(picks, meta.astype(jnp.float32), ((1,), (1,)))
    mine = (owner == me.astype(jnp.float32)) & (within < rows_dev) & (shard == source + nblk)
    mine = mine.astype(jnp.float32)
    before = (iota((held, held), 0) < iota((held, held), 1)).astype(jnp.float32)
    rank = exact_dot(mine, before)
    chosen = jnp.where(rank == turn.astype(jnp.float32), mine, 0.0)

    far = meta - offset
    far = jnp.where(far < 0, far + total_rows, far)
    far = jnp.where(far >= total_rows, far - total_rows, far)
    live = (meta >= 0) & (far < window) & (iota(meta.shape, 1) < stored)
    near = jnp.where(live, far + 1, 0).astype(jnp.float32)

    left = exact_dot(chosen, near)
    partner = jnp.sum(jnp.where(lane == item, left, 0.0), axis=1, keepdims=True)
    partner = partner.astype(jnp.int32) - 1
    right = exact_dot(((index == partner) & (within < rows_dev)).astype(jnp.float32), near)
    found = jnp.full((results, LANES), -1, jnp.int32)
    for i in range(stored):
        found = jnp.where((right == left[:, i : i + 1]) & (right > 0), i, found)
    match = found >= 0
    ahead = (iota((LANES, LANES), 0) < iota((LANES, LANES), 1)).astype(jnp.float32)
    place = exact_dot(match.astype(jnp.float32), ahead).astype(jnp.int32)
    place = jnp.where(match, place, -1)
    left_row = jnp.sum(chosen * index.astype(jnp.float32), axis=1, keepdims=True)
    code = left_row.astype(jnp.int32) * stored + found
    code += (partner * stored + lane) << SHIFT
    pairs = jnp.full((results, LANES), window * stored, jnp.int32)
    for u in range(stored):
        pairs = jnp.where(place[:, u : u + 1] == lane, code[:, u : u + 1], pairs)
    count = jnp.sum(match.astype(jnp.float32), axis=1, keepdims=True).astype(jnp.int32)
    return jnp.where(lane == LANES - 1, count, pairs)


def product_kernel(
    dims, near_ref, panel_hbm, out_ref, panel, lists, pairs_ref, sem, list_sem
):
    nblk, ngroups, rows_dev, stored = dims
    slot = pl.program_id(0)
    width = panel.shape[1]
    total = panel_hbm.shape[0]

    @pl.when(slot == 0)
    def _():
        fetch = pltpu.make_async_copy(panel_hbm, panel.at[pl.ds(0, total)], sem)
        fetch.start()
        panel[total] = jnp.zeros((width, width), panel.dtype)
        group_rows = nblk * rows_dev
        lists[...] = work_lists(
            near_ref[...],
            lax.axis_index("blk"),
            (lax.axis_index("cols") - 1) * group_rows,
            ngroups * group_rows,
            rows_dev,
            stored,
            nblk,
        )
        send = pltpu.make_async_copy(lists, pairs_ref, list_sem)
        send.start()
        send.wait()
        fetch.wait()

    bunches = stored // TOGETHER

    def one_bunch(bunch, carry):
        first = bunch * TOGETHER
        most = 0
        for n in range(TOGETHER):
            most = jnp.maximum(most, pairs_ref[slot * stored + first + n, LANES - 1])

        def step(trip, sums):
            new = []
            for n in range(TOGETHER):
                lefts, rights = [], []
                for d in range(DEPTH):
                    code = pairs_ref[slot * stored + first + n, trip * DEPTH + d]
                    lefts.append(panel[code & ((1 << SHIFT) - 1)])
                    rights.append(panel[code >> SHIFT])
                new.append(
                    sums[n]
                    + lax.dot_general(
                        jnp.concatenate(lefts, axis=1),
                        jnp.concatenate(rights, axis=1),
                        (((1,), (1,)), ((), ())),
                        preferred_element_type=jnp.float32,
                    )
                )
            return tuple(new)

        zero = jnp.zeros((width, width), jnp.float32)
        trips = (most + DEPTH - 1) // DEPTH
        sums = lax.fori_loop(0, trips, step, (zero,) * TOGETHER)
        for n in range(TOGETHER):
            out_ref[0, 0, 0, first + n] = sums[n].astype(out_ref.dtype)
        return carry

    lax.fori_loop(0, bunches, one_bunch, 0)


def products(panel, near, nblk, ngroups, rows_dev, stored):
    total, width = panel.shape[0], panel.shape[1]
    slots = nblk * CAP
    return pl.pallas_call(
        functools.partial(product_kernel, (nblk, ngroups, rows_dev, stored)),
        out_shape=jax.ShapeDtypeStruct((1, 1, slots, stored, width, width), panel.dtype),
        grid=(slots,),
        in_specs=[
            pl.BlockSpec(near.shape, lambda slot: (0, 0)),
            pl.BlockSpec(memory_space=pl.ANY),
        ],
        out_specs=pl.BlockSpec(
            (1, 1, 1, stored, width, width), lambda slot: (0, 0, slot, 0, 0, 0)
        ),
        scratch_shapes=[
            pltpu.VMEM((total + 1, width, width), panel.dtype),
            pltpu.VMEM((slots * stored, LANES), jnp.int32),
            pltpu.SMEM((slots * stored, LANES), jnp.int32),
            pltpu.SemaphoreType.DMA,
            pltpu.SemaphoreType.DMA,
        ],
        compiler_params=pltpu.CompilerParams(vmem_limit_bytes=50 * 1024 * 1024),
        name="products",
    )(near, panel)


def local(blocks, columns, counts, owners, *, nblk, ngroups):
    rows_dev, stored, width = blocks.shape[1:4]
    group_rows = nblk * rows_dev
    slot_iota = jnp.arange(stored, dtype=jnp.int32)
    marked = jnp.where(slot_iota[None, None, :] < counts[:, :, None], columns, -1)
    meta = jnp.concatenate([marked[0], owners[0]], axis=1)
    meta = jnp.pad(
        meta, ((0, ROWS - rows_dev), (0, LANES - stored - 1)), constant_values=-1
    )
    panel, near = gather_panel(blocks, meta, ngroups, group_rows)
    panel = panel.reshape(3 * group_rows * stored, width, width)
    near = near.reshape(3 * nblk * ROWS, LANES)
    return products(panel, near, nblk, ngroups, rows_dev, stored)


def solution(mesh):
    placed = (
        P("cols", "blk", None, None, None),
        P("cols", "blk", None),
        P("cols", "blk"),
        P("cols", "blk", None),
    )
    return jax.shard_map(
        functools.partial(local, nblk=mesh.shape["blk"], ngroups=mesh.shape["cols"]),
        mesh=mesh,
        in_specs=placed,
        out_specs=P("cols", "blk", None, None, None, None),
        check_vma=False,
    )
```

```python
import functools

import jax
import jax.numpy as jnp
from jax import lax
from jax.experimental import pallas as pl
from jax.experimental.pallas import tpu as pltpu
from jax.sharding import PartitionSpec as P

CAP = 2
DEPTH = 4
TOGETHER = 4
SHIFT = 12
ROWS, LANES = 8, 128
SPLIT = 1
WINDOW = 2
CYCLE = 2
VIA_PAIR = 1
VIA_FAR = 1
MESH = pl.DeviceIdType.MESH

OWN, PAIR, FAR = 0, 1, 2


def gather_kernel(
    ngroups, rows_dev, blocks_ref, meta_ref, panel_ref, near_ref, send_sem, recv_sem, own_sem
):
    g = lax.axis_index("cols")
    j = lax.axis_index("blk")
    odd = g % 2
    core = j % 2
    side = j // 2
    pair = g + 1 - 2 * odd
    ahead = (g + 2 - 4 * odd + ngroups) % ngroups
    behind = (g - 2 + 4 * odd + ngroups) % ngroups
    slab = {OWN: 1, PAIR: 2 - 2 * odd, FAR: 2 * odd}
    member = {
        0: j,
        1: side * 2 + 1 - core,
        2: (1 - side) * 2 + core,
        3: (1 - side) * 2 + 1 - core,
    }
    device = {
        "core": (g, member[1]),
        "side": (g, member[2]),
        "pair": (pair, j),
        "ahead": (ahead, j),
    }

    barrier = pltpu.get_barrier_semaphore()
    partners = list(device.values()) + [(behind, j)]
    for to_g, to_j in partners:
        pl.semaphore_signal(
            barrier, inc=1, device_id={"cols": to_g, "blk": to_j}, device_id_type=MESH
        )
    pl.semaphore_wait(barrier, len(partners))

    pending = []

    def place(kind, who, m):
        if m == rows_dev:
            return near_ref.at[slab[kind], member[who]]
        return panel_ref.at[slab[kind], member[who] * rows_dev + m]

    def copy(kind, who, m, to, there_kind, there_who):
        slab_there = slab[FAR] if to in ("pair", "ahead") else slab[kind]
        if m == rows_dev:
            mine, there = meta_ref, near_ref.at[slab_there, member[who]]
        else:
            mine = blocks_ref.at[0, m]
            there = panel_ref.at[slab_there, member[who] * rows_dev + m]
        src = mine if (kind, who) == (OWN, 0) else place(kind, who, m)
        to_g, to_j = device[to]
        made = pltpu.make_async_remote_copy(
            src_ref=src,
            dst_ref=there,
            send_sem=send_sem.at[there_kind, there_who, m],
            recv_sem=recv_sem.at[there_kind, there_who, m],
            device_id={"cols": to_g, "blk": to_j},
            device_id_type=MESH,
        )
        made.start()
        pending.append(made)

    def arrived(kind, who, m):
        pltpu.make_async_copy(
            place(kind, who, m), place(kind, who, m), recv_sem.at[kind, who, m]
        ).wait()

    order = [rows_dev] + list(range(rows_dev))
    later = list(order)

    def launch():
        if later:
            m = later.pop(0)
            copy(OWN, 0, m, "pair", PAIR, 0)
            copy(OWN, 0, m, "side", OWN, 2)
            copy(OWN, 0, m, "core", OWN, 1)

    for _ in range(WINDOW + 1):
        launch()
    local_copies = [
        pltpu.make_async_copy(
            blocks_ref.at[0], panel_ref.at[1, pl.ds(j * rows_dev, rows_dev)], own_sem.at[0]
        ),
        pltpu.make_async_copy(meta_ref, near_ref.at[1, j], own_sem.at[1]),
    ]
    for made in local_copies:
        made.start()

    def first(m):
        arrived(PAIR, 0, m)
        copy(PAIR, 0, m, "ahead", FAR, 0)
        if m % CYCLE >= VIA_PAIR:
            copy(PAIR, 0, m, "side", PAIR, 2)
        copy(PAIR, 0, m, "core", PAIR, 1)
        arrived(OWN, 2, m)
        if m % CYCLE < VIA_PAIR:
            copy(OWN, 2, m, "pair", PAIR, 2)
        copy(OWN, 2, m, "core", OWN, 3)
        if m != rows_dev:
            launch()

    def second(m):
        arrived(FAR, 0, m)
        if m % CYCLE >= VIA_FAR:
            copy(FAR, 0, m, "side", FAR, 2)
        copy(FAR, 0, m, "core", FAR, 1)
        arrived(PAIR, 2, m)
        if m % CYCLE < VIA_FAR:
            copy(PAIR, 2, m, "ahead", FAR, 2)
        copy(PAIR, 2, m, "core", PAIR, 3)

    def third(m):
        arrived(FAR, 2, m)
        copy(FAR, 2, m, "core", FAR, 3)

    for step in range(len(order) + 2):
        for back, stage in enumerate((first, second, third)):
            if 0 <= step - back < len(order):
                stage(order[step - back])
    for kind in (OWN, PAIR, FAR):
        for who in (1, 3):
            for m in order:
                arrived(kind, who, m)
    for made in pending:
        made.wait_send()
    for made in local_copies:
        made.wait()


def gather_panel(blocks, meta, ngroups, group_rows):
    rows_dev, stored, width = blocks.shape[1:4]
    return pl.pallas_call(
        functools.partial(gather_kernel, ngroups, rows_dev),
        out_shape=(
            jax.ShapeDtypeStruct((3, group_rows, stored, width, width), blocks.dtype),
            jax.ShapeDtypeStruct((3, group_rows // rows_dev) + meta.shape, meta.dtype),
        ),
        in_specs=[pl.BlockSpec(memory_space=pl.ANY)] * 2,
        out_specs=[pl.BlockSpec(memory_space=pl.ANY)] * 2,
        scratch_shapes=[
            pltpu.SemaphoreType.DMA((3, 4, rows_dev + 1)),
            pltpu.SemaphoreType.DMA((3, 4, rows_dev + 1)),
            pltpu.SemaphoreType.DMA((2,)),
        ],
        compiler_params=pltpu.CompilerParams(collective_id=0, has_side_effects=True),
        name="gather_panel",
    )(blocks, meta)


def exact_dot(left, right, dims=((1,), (0,))):
    return lax.dot_general(
        left.astype(jnp.bfloat16),
        right.astype(jnp.bfloat16),
        (dims, ((), ())),
        preferred_element_type=jnp.float32,
    )


def work_lists(meta, me, offset, total_rows, rows_dev, stored, nblk):
    held = meta.shape[0]
    window = 3 * nblk * rows_dev
    results = nblk * CAP * stored
    bits = ROWS.bit_length() - 1

    def iota(shape, axis):
        return lax.broadcasted_iota(jnp.int32, shape, axis)

    row = iota((results, 1), 0)
    slot = jnp.zeros_like(row)
    for k in range(1, nblk * CAP):
        slot += (row >= k * stored).astype(jnp.int32)
    source = jnp.zeros_like(row)
    for k in range(1, nblk):
        source += (slot >= k * CAP).astype(jnp.int32)
    turn = slot - CAP * source
    item = row - slot * stored
    lane = iota((results, LANES), 1)
    at = iota((results, held), 1)
    shard = at >> bits
    within = at & (ROWS - 1)
    index = shard * rows_dev + within

    picks = (lane == stored).astype(jnp.float32)
    owner = exact_dot(picks, meta.astype(jnp.float32), ((1,), (1,)))
    mine = (owner == me.astype(jnp.float32)) & (within < rows_dev) & (shard == source + nblk)
    mine = mine.astype(jnp.float32)
    before = (iota((held, held), 0) < iota((held, held), 1)).astype(jnp.float32)
    rank = exact_dot(mine, before)
    chosen = jnp.where(rank == turn.astype(jnp.float32), mine, 0.0)

    far = meta - offset
    far = jnp.where(far < 0, far + total_rows, far)
    far = jnp.where(far >= total_rows, far - total_rows, far)
    live = (meta >= 0) & (far < window) & (iota(meta.shape, 1) < stored)
    near = jnp.where(live, far + 1, 0).astype(jnp.float32)

    left = exact_dot(chosen, near)
    partner = jnp.sum(jnp.where(lane == item, left, 0.0), axis=1, keepdims=True)
    partner = partner.astype(jnp.int32) - 1
    right = exact_dot(((index == partner) & (within < rows_dev)).astype(jnp.float32), near)
    found = jnp.full((results, LANES), -1, jnp.int32)
    for i in range(stored):
        found = jnp.where((right == left[:, i : i + 1]) & (right > 0), i, found)
    match = found >= 0
    ahead = (iota((LANES, LANES), 0) < iota((LANES, LANES), 1)).astype(jnp.float32)
    place = exact_dot(match.astype(jnp.float32), ahead).astype(jnp.int32)
    place = jnp.where(match, place, -1)
    left_row = jnp.sum(chosen * index.astype(jnp.float32), axis=1, keepdims=True)
    code = left_row.astype(jnp.int32) * stored + found
    code += (partner * stored + lane) << SHIFT
    pairs = jnp.full((results, LANES), window * stored, jnp.int32)
    for u in range(stored):
        pairs = jnp.where(place[:, u : u + 1] == lane, code[:, u : u + 1], pairs)
    count = jnp.sum(match.astype(jnp.float32), axis=1, keepdims=True).astype(jnp.int32)
    return jnp.where(lane == LANES - 1, count, pairs)


def product_kernel(
    dims, near_ref, panel_hbm, out_ref, panel, lists, pairs_ref, sem, list_sem
):
    nblk, ngroups, rows_dev, stored = dims
    slot = pl.program_id(0)
    width = panel.shape[1]
    total = panel_hbm.shape[0]

    @pl.when(slot == 0)
    def _():
        fetch = pltpu.make_async_copy(panel_hbm, panel.at[pl.ds(0, total)], sem)
        fetch.start()
        panel[total] = jnp.zeros((width, width), panel.dtype)
        group_rows = nblk * rows_dev
        lists[...] = work_lists(
            near_ref[...],
            lax.axis_index("blk"),
            (lax.axis_index("cols") - 1) * group_rows,
            ngroups * group_rows,
            rows_dev,
            stored,
            nblk,
        )
        send = pltpu.make_async_copy(lists, pairs_ref, list_sem)
        send.start()
        send.wait()
        fetch.wait()

    bunches = stored // TOGETHER

    def one_bunch(bunch, carry):
        first = bunch * TOGETHER
        most = 0
        for n in range(TOGETHER):
            most = jnp.maximum(most, pairs_ref[slot * stored + first + n, LANES - 1])

        def step(trip, sums):
            new = []
            for n in range(TOGETHER):
                lefts, rights = [], []
                for d in range(DEPTH):
                    code = pairs_ref[slot * stored + first + n, trip * DEPTH + d]
                    lefts.append(panel[code & ((1 << SHIFT) - 1)])
                    rights.append(panel[code >> SHIFT])
                new.append(
                    sums[n]
                    + lax.dot_general(
                        jnp.concatenate(lefts, axis=1),
                        jnp.concatenate(rights, axis=1),
                        (((1,), (1,)), ((), ())),
                        preferred_element_type=jnp.float32,
                    )
                )
            return tuple(new)

        zero = jnp.zeros((width, width), jnp.float32)
        trips = (most + DEPTH - 1) // DEPTH
        sums = lax.fori_loop(0, trips, step, (zero,) * TOGETHER)
        for n in range(TOGETHER):
            out_ref[0, 0, 0, first + n] = sums[n].astype(out_ref.dtype)
        return carry

    lax.fori_loop(0, bunches, one_bunch, 0)


def products(panel, near, nblk, ngroups, rows_dev, stored):
    total, width = panel.shape[0], panel.shape[1]
    slots = nblk * CAP
    return pl.pallas_call(
        functools.partial(product_kernel, (nblk, ngroups, rows_dev, stored)),
        out_shape=jax.ShapeDtypeStruct((1, 1, slots, stored, width, width), panel.dtype),
        grid=(slots,),
        in_specs=[
            pl.BlockSpec(near.shape, lambda slot: (0, 0)),
            pl.BlockSpec(memory_space=pl.ANY),
        ],
        out_specs=pl.BlockSpec(
            (1, 1, 1, stored, width, width), lambda slot: (0, 0, slot, 0, 0, 0)
        ),
        scratch_shapes=[
            pltpu.VMEM((total + 1, width, width), panel.dtype),
            pltpu.VMEM((slots * stored, LANES), jnp.int32),
            pltpu.SMEM((slots * stored, LANES), jnp.int32),
            pltpu.SemaphoreType.DMA,
            pltpu.SemaphoreType.DMA,
        ],
        compiler_params=pltpu.CompilerParams(vmem_limit_bytes=50 * 1024 * 1024),
        name="products",
    )(near, panel)


def local(blocks, columns, counts, owners, *, nblk, ngroups):
    rows_dev, stored, width = blocks.shape[1:4]
    group_rows = nblk * rows_dev
    slot_iota = jnp.arange(stored, dtype=jnp.int32)
    marked = jnp.where(slot_iota[None, None, :] < counts[:, :, None], columns, -1)
    meta = jnp.concatenate([marked[0], owners[0]], axis=1)
    meta = jnp.pad(
        meta, ((0, ROWS - rows_dev), (0, LANES - stored - 1)), constant_values=-1
    )
    pieces = blocks.reshape(1, rows_dev * SPLIT, stored // SPLIT, width, width)
    panel, near = gather_panel(pieces, meta, ngroups, group_rows * SPLIT)
    panel = panel.reshape(3 * group_rows * stored, width, width)
    near = near.reshape(3 * nblk * ROWS, LANES)
    return products(panel, near, nblk, ngroups, rows_dev, stored)


def solution(mesh):
    placed = (
        P("cols", "blk", None, None, None),
        P("cols", "blk", None),
        P("cols", "blk"),
        P("cols", "blk", None),
    )
    return jax.shard_map(
        functools.partial(local, nblk=mesh.shape["blk"], ngroups=mesh.shape["cols"]),
        mesh=mesh,
        in_specs=placed,
        out_specs=P("cols", "blk", None, None, None, None),
        check_vma=False,
    )
```

```python
import functools

import jax
import jax.numpy as jnp
from jax import lax
from jax.experimental import pallas as pl
from jax.experimental.pallas import tpu as pltpu
from jax.sharding import PartitionSpec as P

CAP = 2
DEPTH = 8
TOGETHER = 4
SHIFT = 12
ROWS, LANES = 8, 128
SPLIT = 1
WINDOW = 2
CYCLE = 2
VIA_PAIR = 1
VIA_FAR = 1
MESH = pl.DeviceIdType.MESH

OWN, PAIR, FAR = 0, 1, 2


def gather_kernel(
    ngroups, rows_dev, blocks_ref, meta_ref, panel_ref, near_ref, send_sem, recv_sem, own_sem
):
    g = lax.axis_index("cols")
    j = lax.axis_index("blk")
    odd = g % 2
    core = j % 2
    side = j // 2
    pair = g + 1 - 2 * odd
    ahead = (g + 2 - 4 * odd + ngroups) % ngroups
    behind = (g - 2 + 4 * odd + ngroups) % ngroups
    slab = {OWN: 1, PAIR: 2 - 2 * odd, FAR: 2 * odd}
    member = {
        0: j,
        1: side * 2 + 1 - core,
        2: (1 - side) * 2 + core,
        3: (1 - side) * 2 + 1 - core,
    }
    device = {
        "core": (g, member[1]),
        "side": (g, member[2]),
        "pair": (pair, j),
        "ahead": (ahead, j),
    }

    barrier = pltpu.get_barrier_semaphore()
    partners = list(device.values()) + [(behind, j)]
    for to_g, to_j in partners:
        pl.semaphore_signal(
            barrier, inc=1, device_id={"cols": to_g, "blk": to_j}, device_id_type=MESH
        )
    pl.semaphore_wait(barrier, len(partners))

    pending = []

    def place(kind, who, m):
        if m == rows_dev:
            return near_ref.at[slab[kind], member[who]]
        return panel_ref.at[slab[kind], member[who] * rows_dev + m]

    def copy(kind, who, m, to, there_kind, there_who):
        slab_there = slab[FAR] if to in ("pair", "ahead") else slab[kind]
        if m == rows_dev:
            mine, there = meta_ref, near_ref.at[slab_there, member[who]]
        else:
            mine = blocks_ref.at[0, m]
            there = panel_ref.at[slab_there, member[who] * rows_dev + m]
        src = mine if (kind, who) == (OWN, 0) else place(kind, who, m)
        to_g, to_j = device[to]
        made = pltpu.make_async_remote_copy(
            src_ref=src,
            dst_ref=there,
            send_sem=send_sem.at[there_kind, there_who, m],
            recv_sem=recv_sem.at[there_kind, there_who, m],
            device_id={"cols": to_g, "blk": to_j},
            device_id_type=MESH,
        )
        made.start()
        pending.append(made)

    def arrived(kind, who, m):
        pltpu.make_async_copy(
            place(kind, who, m), place(kind, who, m), recv_sem.at[kind, who, m]
        ).wait()

    order = [rows_dev] + list(range(rows_dev))
    later = list(order)

    def launch():
        if later:
            m = later.pop(0)
            copy(OWN, 0, m, "pair", PAIR, 0)
            copy(OWN, 0, m, "side", OWN, 2)
            copy(OWN, 0, m, "core", OWN, 1)

    for _ in range(WINDOW + 1):
        launch()
    local_copies = [
        pltpu.make_async_copy(
            blocks_ref.at[0], panel_ref.at[1, pl.ds(j * rows_dev, rows_dev)], own_sem.at[0]
        ),
        pltpu.make_async_copy(meta_ref, near_ref.at[1, j], own_sem.at[1]),
    ]
    for made in local_copies:
        made.start()

    def first(m):
        arrived(PAIR, 0, m)
        copy(PAIR, 0, m, "ahead", FAR, 0)
        if m % CYCLE >= VIA_PAIR:
            copy(PAIR, 0, m, "side", PAIR, 2)
        copy(PAIR, 0, m, "core", PAIR, 1)
        arrived(OWN, 2, m)
        if m % CYCLE < VIA_PAIR:
            copy(OWN, 2, m, "pair", PAIR, 2)
        copy(OWN, 2, m, "core", OWN, 3)
        if m != rows_dev:
            launch()

    def second(m):
        arrived(FAR, 0, m)
        if m % CYCLE >= VIA_FAR:
            copy(FAR, 0, m, "side", FAR, 2)
        copy(FAR, 0, m, "core", FAR, 1)
        arrived(PAIR, 2, m)
        if m % CYCLE < VIA_FAR:
            copy(PAIR, 2, m, "ahead", FAR, 2)
        copy(PAIR, 2, m, "core", PAIR, 3)

    def third(m):
        arrived(FAR, 2, m)
        copy(FAR, 2, m, "core", FAR, 3)

    for step in range(len(order) + 2):
        for back, stage in enumerate((first, second, third)):
            if 0 <= step - back < len(order):
                stage(order[step - back])
    for kind in (OWN, PAIR, FAR):
        for who in (1, 3):
            for m in order:
                arrived(kind, who, m)
    for made in pending:
        made.wait_send()
    for made in local_copies:
        made.wait()


def gather_panel(blocks, meta, ngroups, group_rows):
    rows_dev, stored, width = blocks.shape[1:4]
    return pl.pallas_call(
        functools.partial(gather_kernel, ngroups, rows_dev),
        out_shape=(
            jax.ShapeDtypeStruct((3, group_rows, stored, width, width), blocks.dtype),
            jax.ShapeDtypeStruct((3, group_rows // rows_dev) + meta.shape, meta.dtype),
        ),
        in_specs=[pl.BlockSpec(memory_space=pl.ANY)] * 2,
        out_specs=[pl.BlockSpec(memory_space=pl.ANY)] * 2,
        scratch_shapes=[
            pltpu.SemaphoreType.DMA((3, 4, rows_dev + 1)),
            pltpu.SemaphoreType.DMA((3, 4, rows_dev + 1)),
            pltpu.SemaphoreType.DMA((2,)),
        ],
        compiler_params=pltpu.CompilerParams(collective_id=0, has_side_effects=True),
        name="gather_panel",
    )(blocks, meta)


def exact_dot(left, right, dims=((1,), (0,))):
    return lax.dot_general(
        left.astype(jnp.bfloat16),
        right.astype(jnp.bfloat16),
        (dims, ((), ())),
        preferred_element_type=jnp.float32,
    )


def work_lists(meta, me, offset, total_rows, rows_dev, stored, nblk):
    held = meta.shape[0]
    window = 3 * nblk * rows_dev
    results = nblk * CAP * stored
    bits = ROWS.bit_length() - 1

    def iota(shape, axis):
        return lax.broadcasted_iota(jnp.int32, shape, axis)

    row = iota((results, 1), 0)
    slot = jnp.zeros_like(row)
    for k in range(1, nblk * CAP):
        slot += (row >= k * stored).astype(jnp.int32)
    source = jnp.zeros_like(row)
    for k in range(1, nblk):
        source += (slot >= k * CAP).astype(jnp.int32)
    turn = slot - CAP * source
    item = row - slot * stored
    lane = iota((results, LANES), 1)
    at = iota((results, held), 1)
    shard = at >> bits
    within = at & (ROWS - 1)
    index = shard * rows_dev + within

    picks = (lane == stored).astype(jnp.float32)
    owner = exact_dot(picks, meta.astype(jnp.float32), ((1,), (1,)))
    mine = (owner == me.astype(jnp.float32)) & (within < rows_dev) & (shard == source + nblk)
    mine = mine.astype(jnp.float32)
    before = (iota((held, held), 0) < iota((held, held), 1)).astype(jnp.float32)
    rank = exact_dot(mine, before)
    chosen = jnp.where(rank == turn.astype(jnp.float32), mine, 0.0)

    far = meta - offset
    far = jnp.where(far < 0, far + total_rows, far)
    far = jnp.where(far >= total_rows, far - total_rows, far)
    live = (meta >= 0) & (far < window) & (iota(meta.shape, 1) < stored)
    near = jnp.where(live, far + 1, 0).astype(jnp.float32)

    left = exact_dot(chosen, near)
    partner = jnp.sum(jnp.where(lane == item, left, 0.0), axis=1, keepdims=True)
    partner = partner.astype(jnp.int32) - 1
    right = exact_dot(((index == partner) & (within < rows_dev)).astype(jnp.float32), near)
    found = jnp.full((results, LANES), -1, jnp.int32)
    for i in range(stored):
        found = jnp.where((right == left[:, i : i + 1]) & (right > 0), i, found)
    match = found >= 0
    ahead = (iota((LANES, LANES), 0) < iota((LANES, LANES), 1)).astype(jnp.float32)
    place = exact_dot(match.astype(jnp.float32), ahead).astype(jnp.int32)
    place = jnp.where(match, place, -1)
    left_row = jnp.sum(chosen * index.astype(jnp.float32), axis=1, keepdims=True)
    code = left_row.astype(jnp.int32) * stored + found
    code += (partner * stored + lane) << SHIFT
    pairs = jnp.full((results, LANES), window * stored, jnp.int32)
    for u in range(stored):
        pairs = jnp.where(place[:, u : u + 1] == lane, code[:, u : u + 1], pairs)
    count = jnp.sum(match.astype(jnp.float32), axis=1, keepdims=True).astype(jnp.int32)
    return jnp.where(lane == LANES - 1, count, pairs)


def product_kernel(
    dims, near_ref, panel_hbm, out_ref, panel, lists, pairs_ref, sem, list_sem
):
    nblk, ngroups, rows_dev, stored = dims
    slot = pl.program_id(0)
    width = panel.shape[1]
    total = panel_hbm.shape[0]

    @pl.when(slot == 0)
    def _():
        fetch = pltpu.make_async_copy(panel_hbm, panel.at[pl.ds(0, total)], sem)
        fetch.start()
        panel[total] = jnp.zeros((width, width), panel.dtype)
        group_rows = nblk * rows_dev
        lists[...] = work_lists(
            near_ref[...],
            lax.axis_index("blk"),
            (lax.axis_index("cols") - 1) * group_rows,
            ngroups * group_rows,
            rows_dev,
            stored,
            nblk,
        )
        send = pltpu.make_async_copy(lists, pairs_ref, list_sem)
        send.start()
        send.wait()
        fetch.wait()

    bunches = stored // TOGETHER

    def one_bunch(bunch, carry):
        first = bunch * TOGETHER
        most = 0
        for n in range(TOGETHER):
            most = jnp.maximum(most, pairs_ref[slot * stored + first + n, LANES - 1])

        def step(trip, sums):
            new = []
            for n in range(TOGETHER):
                lefts, rights = [], []
                for d in range(DEPTH):
                    code = pairs_ref[slot * stored + first + n, trip * DEPTH + d]
                    lefts.append(panel[code & ((1 << SHIFT) - 1)])
                    rights.append(panel[code >> SHIFT])
                new.append(
                    sums[n]
                    + lax.dot_general(
                        jnp.concatenate(lefts, axis=1),
                        jnp.concatenate(rights, axis=1),
                        (((1,), (1,)), ((), ())),
                        preferred_element_type=jnp.float32,
                    )
                )
            return tuple(new)

        zero = jnp.zeros((width, width), jnp.float32)
        trips = (most + DEPTH - 1) // DEPTH
        sums = lax.fori_loop(0, trips, step, (zero,) * TOGETHER)
        for n in range(TOGETHER):
            out_ref[0, 0, 0, first + n] = sums[n].astype(out_ref.dtype)
        return carry

    lax.fori_loop(0, bunches, one_bunch, 0)


def products(panel, near, nblk, ngroups, rows_dev, stored):
    total, width = panel.shape[0], panel.shape[1]
    slots = nblk * CAP
    return pl.pallas_call(
        functools.partial(product_kernel, (nblk, ngroups, rows_dev, stored)),
        out_shape=jax.ShapeDtypeStruct((1, 1, slots, stored, width, width), panel.dtype),
        grid=(slots,),
        in_specs=[
            pl.BlockSpec(near.shape, lambda slot: (0, 0)),
            pl.BlockSpec(memory_space=pl.ANY),
        ],
        out_specs=pl.BlockSpec(
            (1, 1, 1, stored, width, width), lambda slot: (0, 0, slot, 0, 0, 0)
        ),
        scratch_shapes=[
            pltpu.VMEM((total + 1, width, width), panel.dtype),
            pltpu.VMEM((slots * stored, LANES), jnp.int32),
            pltpu.SMEM((slots * stored, LANES), jnp.int32),
            pltpu.SemaphoreType.DMA,
            pltpu.SemaphoreType.DMA,
        ],
        compiler_params=pltpu.CompilerParams(vmem_limit_bytes=50 * 1024 * 1024),
        name="products",
    )(near, panel)


def local(blocks, columns, counts, owners, *, nblk, ngroups):
    rows_dev, stored, width = blocks.shape[1:4]
    group_rows = nblk * rows_dev
    slot_iota = jnp.arange(stored, dtype=jnp.int32)
    marked = jnp.where(slot_iota[None, None, :] < counts[:, :, None], columns, -1)
    meta = jnp.concatenate([marked[0], owners[0]], axis=1)
    meta = jnp.pad(
        meta, ((0, ROWS - rows_dev), (0, LANES - stored - 1)), constant_values=-1
    )
    pieces = blocks.reshape(1, rows_dev * SPLIT, stored // SPLIT, width, width)
    panel, near = gather_panel(pieces, meta, ngroups, group_rows * SPLIT)
    panel = panel.reshape(3 * group_rows * stored, width, width)
    near = near.reshape(3 * nblk * ROWS, LANES)
    return products(panel, near, nblk, ngroups, rows_dev, stored)


def solution(mesh):
    placed = (
        P("cols", "blk", None, None, None),
        P("cols", "blk", None),
        P("cols", "blk"),
        P("cols", "blk", None),
    )
    return jax.shard_map(
        functools.partial(local, nblk=mesh.shape["blk"], ngroups=mesh.shape["cols"]),
        mesh=mesh,
        in_specs=placed,
        out_specs=P("cols", "blk", None, None, None, None),
        check_vma=False,
    )
```

```python
import functools

import jax
import jax.numpy as jnp
from jax import lax
from jax.experimental import pallas as pl
from jax.experimental.pallas import tpu as pltpu
from jax.sharding import PartitionSpec as P

CAP = 2
DEPTH = 12
TOGETHER = 4
SHIFT = 12
ROWS, LANES = 8, 128
SPLIT = 1
WINDOW = 2
CYCLE = 2
VIA_PAIR = 1
VIA_FAR = 1
MESH = pl.DeviceIdType.MESH

OWN, PAIR, FAR = 0, 1, 2


def gather_kernel(
    ngroups, rows_dev, blocks_ref, meta_ref, panel_ref, near_ref, send_sem, recv_sem, own_sem
):
    g = lax.axis_index("cols")
    j = lax.axis_index("blk")
    odd = g % 2
    core = j % 2
    side = j // 2
    pair = g + 1 - 2 * odd
    ahead = (g + 2 - 4 * odd + ngroups) % ngroups
    behind = (g - 2 + 4 * odd + ngroups) % ngroups
    slab = {OWN: 1, PAIR: 2 - 2 * odd, FAR: 2 * odd}
    member = {
        0: j,
        1: side * 2 + 1 - core,
        2: (1 - side) * 2 + core,
        3: (1 - side) * 2 + 1 - core,
    }
    device = {
        "core": (g, member[1]),
        "side": (g, member[2]),
        "pair": (pair, j),
        "ahead": (ahead, j),
    }

    barrier = pltpu.get_barrier_semaphore()
    partners = list(device.values()) + [(behind, j)]
    for to_g, to_j in partners:
        pl.semaphore_signal(
            barrier, inc=1, device_id={"cols": to_g, "blk": to_j}, device_id_type=MESH
        )
    pl.semaphore_wait(barrier, len(partners))

    pending = []

    def place(kind, who, m):
        if m == rows_dev:
            return near_ref.at[slab[kind], member[who]]
        return panel_ref.at[slab[kind], member[who] * rows_dev + m]

    def copy(kind, who, m, to, there_kind, there_who):
        slab_there = slab[FAR] if to in ("pair", "ahead") else slab[kind]
        if m == rows_dev:
            mine, there = meta_ref, near_ref.at[slab_there, member[who]]
        else:
            mine = blocks_ref.at[0, m]
            there = panel_ref.at[slab_there, member[who] * rows_dev + m]
        src = mine if (kind, who) == (OWN, 0) else place(kind, who, m)
        to_g, to_j = device[to]
        made = pltpu.make_async_remote_copy(
            src_ref=src,
            dst_ref=there,
            send_sem=send_sem.at[there_kind, there_who, m],
            recv_sem=recv_sem.at[there_kind, there_who, m],
            device_id={"cols": to_g, "blk": to_j},
            device_id_type=MESH,
        )
        made.start()
        pending.append(made)

    def arrived(kind, who, m):
        pltpu.make_async_copy(
            place(kind, who, m), place(kind, who, m), recv_sem.at[kind, who, m]
        ).wait()

    order = [rows_dev] + list(range(rows_dev))
    later = list(order)

    def launch():
        if later:
            m = later.pop(0)
            copy(OWN, 0, m, "pair", PAIR, 0)
            copy(OWN, 0, m, "side", OWN, 2)
            copy(OWN, 0, m, "core", OWN, 1)

    for _ in range(WINDOW + 1):
        launch()
    local_copies = [
        pltpu.make_async_copy(
            blocks_ref.at[0], panel_ref.at[1, pl.ds(j * rows_dev, rows_dev)], own_sem.at[0]
        ),
        pltpu.make_async_copy(meta_ref, near_ref.at[1, j], own_sem.at[1]),
    ]
    for made in local_copies:
        made.start()

    def first(m):
        arrived(PAIR, 0, m)
        copy(PAIR, 0, m, "ahead", FAR, 0)
        if m % CYCLE >= VIA_PAIR:
            copy(PAIR, 0, m, "side", PAIR, 2)
        copy(PAIR, 0, m, "core", PAIR, 1)
        arrived(OWN, 2, m)
        if m % CYCLE < VIA_PAIR:
            copy(OWN, 2, m, "pair", PAIR, 2)
        copy(OWN, 2, m, "core", OWN, 3)
        if m != rows_dev:
            launch()

    def second(m):
        arrived(FAR, 0, m)
        if m % CYCLE >= VIA_FAR:
            copy(FAR, 0, m, "side", FAR, 2)
        copy(FAR, 0, m, "core", FAR, 1)
        arrived(PAIR, 2, m)
        if m % CYCLE < VIA_FAR:
            copy(PAIR, 2, m, "ahead", FAR, 2)
        copy(PAIR, 2, m, "core", PAIR, 3)

    def third(m):
        arrived(FAR, 2, m)
        copy(FAR, 2, m, "core", FAR, 3)

    for step in range(len(order) + 2):
        for back, stage in enumerate((first, second, third)):
            if 0 <= step - back < len(order):
                stage(order[step - back])
    for kind in (OWN, PAIR, FAR):
        for who in (1, 3):
            for m in order:
                arrived(kind, who, m)
    for made in pending:
        made.wait_send()
    for made in local_copies:
        made.wait()


def gather_panel(blocks, meta, ngroups, group_rows):
    rows_dev, stored, width = blocks.shape[1:4]
    return pl.pallas_call(
        functools.partial(gather_kernel, ngroups, rows_dev),
        out_shape=(
            jax.ShapeDtypeStruct((3, group_rows, stored, width, width), blocks.dtype),
            jax.ShapeDtypeStruct((3, group_rows // rows_dev) + meta.shape, meta.dtype),
        ),
        in_specs=[pl.BlockSpec(memory_space=pl.ANY)] * 2,
        out_specs=[pl.BlockSpec(memory_space=pl.ANY)] * 2,
        scratch_shapes=[
            pltpu.SemaphoreType.DMA((3, 4, rows_dev + 1)),
            pltpu.SemaphoreType.DMA((3, 4, rows_dev + 1)),
            pltpu.SemaphoreType.DMA((2,)),
        ],
        compiler_params=pltpu.CompilerParams(collective_id=0, has_side_effects=True),
        name="gather_panel",
    )(blocks, meta)


def exact_dot(left, right, dims=((1,), (0,))):
    return lax.dot_general(
        left.astype(jnp.bfloat16),
        right.astype(jnp.bfloat16),
        (dims, ((), ())),
        preferred_element_type=jnp.float32,
    )


def work_lists(meta, me, offset, total_rows, rows_dev, stored, nblk):
    held = meta.shape[0]
    window = 3 * nblk * rows_dev
    results = nblk * CAP * stored
    bits = ROWS.bit_length() - 1

    def iota(shape, axis):
        return lax.broadcasted_iota(jnp.int32, shape, axis)

    row = iota((results, 1), 0)
    slot = jnp.zeros_like(row)
    for k in range(1, nblk * CAP):
        slot += (row >= k * stored).astype(jnp.int32)
    source = jnp.zeros_like(row)
    for k in range(1, nblk):
        source += (slot >= k * CAP).astype(jnp.int32)
    turn = slot - CAP * source
    item = row - slot * stored
    lane = iota((results, LANES), 1)
    at = iota((results, held), 1)
    shard = at >> bits
    within = at & (ROWS - 1)
    index = shard * rows_dev + within

    picks = (lane == stored).astype(jnp.float32)
    owner = exact_dot(picks, meta.astype(jnp.float32), ((1,), (1,)))
    mine = (owner == me.astype(jnp.float32)) & (within < rows_dev) & (shard == source + nblk)
    mine = mine.astype(jnp.float32)
    before = (iota((held, held), 0) < iota((held, held), 1)).astype(jnp.float32)
    rank = exact_dot(mine, before)
    chosen = jnp.where(rank == turn.astype(jnp.float32), mine, 0.0)

    far = meta - offset
    far = jnp.where(far < 0, far + total_rows, far)
    far = jnp.where(far >= total_rows, far - total_rows, far)
    live = (meta >= 0) & (far < window) & (iota(meta.shape, 1) < stored)
    near = jnp.where(live, far + 1, 0).astype(jnp.float32)

    left = exact_dot(chosen, near)
    partner = jnp.sum(jnp.where(lane == item, left, 0.0), axis=1, keepdims=True)
    partner = partner.astype(jnp.int32) - 1
    right = exact_dot(((index == partner) & (within < rows_dev)).astype(jnp.float32), near)
    found = jnp.full((results, LANES), -1, jnp.int32)
    for i in range(stored):
        found = jnp.where((right == left[:, i : i + 1]) & (right > 0), i, found)
    match = found >= 0
    ahead = (iota((LANES, LANES), 0) < iota((LANES, LANES), 1)).astype(jnp.float32)
    place = exact_dot(match.astype(jnp.float32), ahead).astype(jnp.int32)
    place = jnp.where(match, place, -1)
    left_row = jnp.sum(chosen * index.astype(jnp.float32), axis=1, keepdims=True)
    code = left_row.astype(jnp.int32) * stored + found
    code += (partner * stored + lane) << SHIFT
    pairs = jnp.full((results, LANES), window * stored, jnp.int32)
    for u in range(stored):
        pairs = jnp.where(place[:, u : u + 1] == lane, code[:, u : u + 1], pairs)
    count = jnp.sum(match.astype(jnp.float32), axis=1, keepdims=True).astype(jnp.int32)
    return jnp.where(lane == LANES - 1, count, pairs)


def product_kernel(
    dims, near_ref, panel_hbm, out_ref, panel, lists, pairs_ref, sem, list_sem
):
    nblk, ngroups, rows_dev, stored = dims
    slot = pl.program_id(0)
    width = panel.shape[1]
    total = panel_hbm.shape[0]

    @pl.when(slot == 0)
    def _():
        fetch = pltpu.make_async_copy(panel_hbm, panel.at[pl.ds(0, total)], sem)
        fetch.start()
        panel[total] = jnp.zeros((width, width), panel.dtype)
        group_rows = nblk * rows_dev
        lists[...] = work_lists(
            near_ref[...],
            lax.axis_index("blk"),
            (lax.axis_index("cols") - 1) * group_rows,
            ngroups * group_rows,
            rows_dev,
            stored,
            nblk,
        )
        send = pltpu.make_async_copy(lists, pairs_ref, list_sem)
        send.start()
        send.wait()
        fetch.wait()

    bunches = stored // TOGETHER

    def one_bunch(bunch, carry):
        first = bunch * TOGETHER
        most = 0
        for n in range(TOGETHER):
            most = jnp.maximum(most, pairs_ref[slot * stored + first + n, LANES - 1])

        def step(trip, sums):
            new = []
            for n in range(TOGETHER):
                lefts, rights = [], []
                for d in range(DEPTH):
                    code = pairs_ref[slot * stored + first + n, trip * DEPTH + d]
                    lefts.append(panel[code & ((1 << SHIFT) - 1)])
                    rights.append(panel[code >> SHIFT])
                new.append(
                    sums[n]
                    + lax.dot_general(
                        jnp.concatenate(lefts, axis=1),
                        jnp.concatenate(rights, axis=1),
                        (((1,), (1,)), ((), ())),
                        preferred_element_type=jnp.float32,
                    )
                )
            return tuple(new)

        zero = jnp.zeros((width, width), jnp.float32)
        trips = (most + DEPTH - 1) // DEPTH
        sums = lax.fori_loop(0, trips, step, (zero,) * TOGETHER)
        for n in range(TOGETHER):
            out_ref[0, 0, 0, first + n] = sums[n].astype(out_ref.dtype)
        return carry

    lax.fori_loop(0, bunches, one_bunch, 0)


def products(panel, near, nblk, ngroups, rows_dev, stored):
    total, width = panel.shape[0], panel.shape[1]
    slots = nblk * CAP
    return pl.pallas_call(
        functools.partial(product_kernel, (nblk, ngroups, rows_dev, stored)),
        out_shape=jax.ShapeDtypeStruct((1, 1, slots, stored, width, width), panel.dtype),
        grid=(slots,),
        in_specs=[
            pl.BlockSpec(near.shape, lambda slot: (0, 0)),
            pl.BlockSpec(memory_space=pl.ANY),
        ],
        out_specs=pl.BlockSpec(
            (1, 1, 1, stored, width, width), lambda slot: (0, 0, slot, 0, 0, 0)
        ),
        scratch_shapes=[
            pltpu.VMEM((total + 1, width, width), panel.dtype),
            pltpu.VMEM((slots * stored, LANES), jnp.int32),
            pltpu.SMEM((slots * stored, LANES), jnp.int32),
            pltpu.SemaphoreType.DMA,
            pltpu.SemaphoreType.DMA,
        ],
        compiler_params=pltpu.CompilerParams(vmem_limit_bytes=50 * 1024 * 1024),
        name="products",
    )(near, panel)


def local(blocks, columns, counts, owners, *, nblk, ngroups):
    rows_dev, stored, width = blocks.shape[1:4]
    group_rows = nblk * rows_dev
    slot_iota = jnp.arange(stored, dtype=jnp.int32)
    marked = jnp.where(slot_iota[None, None, :] < counts[:, :, None], columns, -1)
    meta = jnp.concatenate([marked[0], owners[0]], axis=1)
    meta = jnp.pad(
        meta, ((0, ROWS - rows_dev), (0, LANES - stored - 1)), constant_values=-1
    )
    pieces = blocks.reshape(1, rows_dev * SPLIT, stored // SPLIT, width, width)
    panel, near = gather_panel(pieces, meta, ngroups, group_rows * SPLIT)
    panel = panel.reshape(3 * group_rows * stored, width, width)
    near = near.reshape(3 * nblk * ROWS, LANES)
    return products(panel, near, nblk, ngroups, rows_dev, stored)


def solution(mesh):
    placed = (
        P("cols", "blk", None, None, None),
        P("cols", "blk", None),
        P("cols", "blk"),
        P("cols", "blk", None),
    )
    return jax.shard_map(
        functools.partial(local, nblk=mesh.shape["blk"], ngroups=mesh.shape["cols"]),
        mesh=mesh,
        in_specs=placed,
        out_specs=P("cols", "blk", None, None, None, None),
        check_vma=False,
    )
```
